32 devices in a mesh: pb: 16 (over z, x, core), ka: 2 (over y).
Axes of the slice: x: 2, y: 2, z: 4, core: 2. Of those that a mesh axis runs over, the one named last changes fastest.
Arguments:
- queries: bfloat16 [2048, 2048], P(('pb', 'ka')), may hold values from -8 to 8
- keys: bfloat16 [2048, 128], P(('ka', 'pb')), may hold values from -6 to 6
- values: bfloat16 [2048, 128], P(('ka', 'pb')), may hold values from -6 to 6
- query_pos: int32 [2048], replicated, may hold values from 0 to 2047, as said below
- key_pos: int32 [2048], replicated, may hold values from 0 to 2047, as said below
- block_mask: int32 [32, 32], replicated, may hold values from 0 to 1, as said below
Outputs:
- attended: bfloat16 [2048, 2048], P(('pb', 'ka'))
The draws below stay inside these ranges and needn't reach their ends.
Inputs may be any that keep to these rules, and one draw needn't show every extreme that they name: `query_pos`: query tile u (rows u * 64 to (u + 1) * 64 - 1) holds 64 consecutive positions in increasing order, 0 + r * 64 onward, where the tiles' r are a permutation of 0 to 31. `key_pos`: key tile t (rows t * 64 to (t + 1) * 64 - 1) holds 64 consecutive positions in increasing order, r * 64 onward, where the tiles' r are a permutation of 0 to 31. `block_mask`: every query tile may attend to the key tile that holds position 0.
All inputs are finite; a program needn't handle non-finite values.
Results may differ from the reference program's by a relative error of at most 0.0015.
Values may be sent and summed in bfloat16 or wider, within the bound.
No kernel may reach another device: no remote copies, remote signals or barrier semaphores. Data moves between devices by JAX's collectives and lax.ppermute only.
A program may use at most 128 MiB of HBM per device.

```python
import jax
import jax.numpy as jnp
from jax import lax

H = 16
HD = 128
Q_DEV = 64
K_DEV = 64
QUERIES = 2048
KEYS = 2048


def layout_runs(key):
    query_runs = jax.random.permutation(jax.random.fold_in(key, 101), QUERIES // Q_DEV).astype(jnp.int32)
    key_runs = jax.random.permutation(jax.random.fold_in(key, 102), KEYS // K_DEV).astype(jnp.int32)
    return (query_runs, key_runs)


def draw_query_pos(key, part):
    query_runs, key_runs = layout_runs(key)
    offsets = jnp.arange(Q_DEV, dtype=jnp.int32)
    positions = KEYS - QUERIES + query_runs[:, None] * Q_DEV + offsets[None, :]
    return positions.reshape(QUERIES).astype(jnp.int32)


def draw_key_pos(key, part):
    query_runs, key_runs = layout_runs(key)
    offsets = jnp.arange(K_DEV, dtype=jnp.int32)
    positions = key_runs[:, None] * K_DEV + offsets[None, :]
    return positions.reshape(KEYS).astype(jnp.int32)


def draw_block_mask(key, part):
    query_runs, key_runs = layout_runs(key)
    coins = jax.random.randint(jax.random.fold_in(key, 103), (QUERIES // Q_DEV, KEYS // K_DEV), 0, 5)
    forced = (key_runs == 0)[None, :]
    return ((coins < 3) | forced).astype(jnp.int32)


def draw_keys(key, part):
    base = jnp.clip(jax.random.normal(jax.random.fold_in(key, 201), (KEYS, HD), jnp.float32), -6.0, 6.0)
    return base.astype(jnp.bfloat16)


def draw_queries(key, part):
    base = 2.5 * jax.random.normal(jax.random.fold_in(key, 202), (QUERIES, H * HD), jnp.float32)
    return jnp.clip(base, -8.0, 8.0).astype(jnp.bfloat16)


def block_levels(key, dims, cuts, low, high):
    factor_of, own = 1.0, jax.random.fold_in(key, 6)
    for position, blocks in cuts:
        draws = jnp.exp(jax.random.uniform(jax.random.fold_in(own, position), (blocks,), jnp.float32, low / len(cuts), high / len(cuts)))
        factor_of = factor_of * jnp.repeat(draws, dims[position] // blocks).reshape([-1 if axis == position else 1 for axis in range(len(dims))])
    return factor_of


def normal_values(own_key, dims, deviation, bound, cuts=(), kind=jnp.bfloat16):
    level = block_levels(own_key, dims, cuts, -0.22, 0.18) if cuts else 1.0
    result = jax.random.normal(own_key, dims, jnp.float32) * deviation * level
    return jnp.minimum(jnp.maximum(result, -bound), bound).astype(kind)


def setup_inputs(seed: int = 0) -> dict:
    key_of = jax.random.split(jax.random.key(seed), 7)
    queries = draw_queries(jax.random.fold_in(key_of[6], 71), 0)
    keys = draw_keys(jax.random.fold_in(key_of[6], 71), 0)
    values = normal_values(key_of[2], (KEYS, HD), 1.0, 6.0, ((0, 32),))
    query_pos = draw_query_pos(jax.random.fold_in(key_of[6], 71), 0)
    key_pos = draw_key_pos(jax.random.fold_in(key_of[6], 71), 0)
    block_mask = draw_block_mask(jax.random.fold_in(key_of[6], 71), 0)
    return dict(queries=queries, keys=keys, values=values, query_pos=query_pos, key_pos=key_pos, block_mask=block_mask)


NEG = -1.0e30


def reference(queries, keys, values, query_pos, key_pos, block_mask):
    rows = min(128, QUERIES)
    count = QUERIES // rows
    key_tile = jnp.arange(KEYS, dtype=jnp.int32) // K_DEV
    scale = HD ** -0.5
    values_wide = values.astype(jnp.float32)

    def one_block(index):
        start = (index * rows).astype(jnp.int32)
        q_rows = lax.dynamic_slice_in_dim(queries, start, rows, 0).reshape(rows * H, HD)
        q_pos = lax.dynamic_slice_in_dim(query_pos, start, rows, 0)
        q_tile = (start + jnp.arange(rows, dtype=jnp.int32)) // Q_DEV
        tile_ok = block_mask[q_tile][:, key_tile]
        allowed = (key_pos[None, :] <= q_pos[:, None]) & (tile_ok > 0)
        scores = jnp.dot(q_rows, keys.T, preferred_element_type=jnp.float32) * scale
        scores = scores.reshape(rows, H, KEYS)
        top = jnp.max(jnp.where(allowed[:, None, :], scores, NEG), axis=-1)
        weights = jnp.where(allowed[:, None, :], jnp.exp(scores - top[..., None]), 0.0)
        total = jnp.sum(weights, axis=-1)
        summed = jnp.dot(weights.reshape(rows * H, KEYS), values_wide, precision=lax.Precision.HIGHEST)
        summed = summed.reshape(rows, H, HD)
        return (summed / total[..., None]).reshape(rows, H * HD).astype(jnp.bfloat16)

    blocks = lax.map(one_block, jnp.arange(count, dtype=jnp.int32))
    return blocks.reshape(QUERIES, H * HD)
```

```python
import functools
import math

import jax
import jax.numpy as jnp
from jax import lax
from jax.experimental import pallas as pl
from jax.experimental.pallas import tpu as pltpu
from jax.sharding import PartitionSpec as P

NEG = -1e30
CHUNK_TILES = 4
SCORE_BYTES = 16 * 2**20


def swap(x, step, n_devices):
    return lax.ppermute(x, ("pb", "ka"), [(i, i ^ step) for i in range(n_devices)])


def gather_rounds(n_pb, n_ka):
    core = n_ka if n_pb > 1 else 0
    bits = [1 << b for b in range((n_pb * n_ka).bit_length() - 1)]
    bits = [b for b in bits if b != core]
    low = [b for b in bits if b < 4 * n_ka]
    high = [b for b in bits if b >= 4 * n_ka]
    rounds = []
    for group in (high, low):
        while group:
            pair, group = group[:2], group[2:]
            rounds.append([pair[0], pair[1], pair[0] ^ pair[1]] if len(pair) == 2 else pair)
    if core:
        rounds.append([core])
    return rounds


def gather(x, rounds, n_devices):
    steps = [0]
    for group in rounds:
        x = jnp.concatenate([x] + [swap(x, step, n_devices) for step in group], 0)
        steps = [s ^ g for g in [0] + group for s in steps]
    return x, steps


def kernel(
    steps, k_dev, width, heads, rows_block,
    me_ref, ok_ref, first_ref, q_ref, kv_ref, out_ref,
    qs, kc, vc, scores, best, acc,
):
    q_dev = q_ref.shape[0]
    tiles = len(steps)
    chunk = CHUNK_TILES * k_dev
    slots = kc.shape[0] // k_dev
    mine = me_ref[0]
    q_first = me_ref[1]

    for h in range(heads):
        qs[h * q_dev : (h + 1) * q_dev, :] = q_ref[:, h * width : (h + 1) * width]
    vc[:, width:] = jnp.ones((slots * k_dev, vc.shape[1] - width), vc.dtype)

    def put(slot, at):
        rows = pl.ds(pl.multiple_of(at * k_dev, k_dev), k_dev)
        kc[rows, :] = kv_ref[slot * k_dev : (slot + 1) * k_dev, :width]
        vc[rows, :width] = kv_ref[slot * k_dev : (slot + 1) * k_dev, width:]

    at = jnp.int32(slots - 1)
    diagonal = jnp.int32(0)
    for slot, step in enumerate(steps):
        tile = mine ^ step
        first = first_ref[tile]
        ok = ok_ref[tile] == 1
        put(slot, at)
        at = jnp.where(ok & (first < q_first), at - 1, at)
        diagonal = jnp.where(ok & (first == q_first), slot + 1, diagonal)
    has_diagonal = diagonal > 0

    @pl.when(has_diagonal)
    def _():
        source = pl.ds(pl.multiple_of((diagonal - 1) * k_dev, k_dev), k_dev)
        rows = pl.ds(pl.multiple_of(at * k_dev, k_dev), k_dev)
        kc[rows, :] = kv_ref[source, :width]
        vc[rows, :width] = kv_ref[source, width:]

    start = jnp.where(has_diagonal, at, at + 1)
    first_chunk = start // CHUNK_TILES
    pad = start - first_chunk * CHUNK_TILES
    n_chunks = slots // CHUNK_TILES - first_chunk
    for j in range(CHUNK_TILES - 1):
        @pl.when(j < pad)
        def _():
            rows = pl.ds(pl.multiple_of((first_chunk * CHUNK_TILES + j) * k_dev, k_dev), k_dev)
            vc[rows, :width] = jnp.zeros((k_dev, width), vc.dtype)

    lane = lax.broadcasted_iota(jnp.int32, (q_dev, chunk), 1)
    lane_tile = lane // k_dev
    bias = jnp.where(lane_tile < pad, k_dev, -k_dev)
    bias = jnp.where((lane_tile == pad) & has_diagonal, 0, bias)
    allowed = lane % k_dev + bias <= lax.broadcasted_iota(jnp.int32, (q_dev, chunk), 0)
    allowed = jnp.concatenate([allowed] * (rows_block // q_dev), 0)

    n_blocks = heads * q_dev // rows_block
    factor = width ** (-0.5) * math.log2(math.e)

    def rows_of(c):
        return pl.ds(pl.multiple_of((first_chunk + c) * chunk, chunk), chunk)

    def score(block, c):
        s = lax.dot_general(
            qs[block * rows_block : (block + 1) * rows_block, :], kc[rows_of(c), :],
            (((1,), (1,)), ((), ())), preferred_element_type=jnp.float32,
        )
        return s

    def keep(block, c, s):
        scores[block % 2, c] = s
        m = s[:, :128]
        for j in range(1, chunk // 128):
            m = jnp.maximum(m, s[:, j * 128 : (j + 1) * 128])
        return m

    def weigh(block, c, top):
        p = jnp.exp2((scores[block % 2, c] - top) * factor)
        high = p.astype(jnp.bfloat16)
        low = (p - high.astype(jnp.float32)).astype(jnp.bfloat16)
        v = vc[rows_of(c), :]
        return jnp.dot(
            jnp.concatenate([high, low], 1), jnp.concatenate([v, v], 0),
            preferred_element_type=jnp.float32,
        )

    best[0] = keep(0, 0, jnp.where(allowed, score(0, 0), NEG))

    @pl.loop(1, n_chunks)
    def _(c):
        best[0] = jnp.maximum(best[0], keep(0, c, score(0, c)))

    for block in range(n_blocks):
        now, later = block % 2, (block + 1) % 2
        top = jnp.max(best[now], axis=1, keepdims=True)
        top = jnp.broadcast_to(top, (rows_block, 128))
        best[now] = top
        wide = jnp.concatenate([top] * (chunk // 128), 1)
        acc[...] = weigh(block, 0, wide)
        if block + 1 < n_blocks:
            best[later] = keep(block + 1, 0, jnp.where(allowed, score(block + 1, 0), NEG))

        @pl.loop(1, n_chunks)
        def _(c):
            wide = jnp.concatenate([best[now]] * (chunk // 128), 1)
            acc[...] += weigh(block, c, wide)
            if block + 1 < n_blocks:
                best[later] = jnp.maximum(best[later], keep(block + 1, c, score(block + 1, c)))

        for j in range(rows_block // q_dev):
            h = block * (rows_block // q_dev) + j
            part = acc[j * q_dev : (j + 1) * q_dev, :]
            out_ref[:, h * width : (h + 1) * width] = (
                part[:, :width] / part[:, width:]
            ).astype(out_ref.dtype)


def attend(queries, kv, me, ok, first, steps, k_dev):
    q_dev, columns = queries.shape
    width = kv.shape[1] // 2
    heads = columns // width
    tiles = len(steps)
    slots = -(-(tiles + 1) // CHUNK_TILES) * CHUNK_TILES
    chunk = CHUNK_TILES * k_dev
    heads_block = max(1, heads // 2)
    while heads_block > 1 and 2 * heads_block * q_dev * slots * k_dev * 4 > SCORE_BYTES:
        heads_block //= 2
    rows_block = heads_block * q_dev
    smem = pl.BlockSpec(memory_space=pltpu.SMEM)
    vmem = pl.BlockSpec(memory_space=pltpu.VMEM)
    return pl.pallas_call(
        functools.partial(kernel, steps, k_dev, width, heads, rows_block),
        out_shape=jax.ShapeDtypeStruct(queries.shape, jnp.bfloat16),
        in_specs=[smem, smem, smem, vmem, vmem],
        out_specs=vmem,
        scratch_shapes=[
            pltpu.VMEM((heads * q_dev, width), jnp.bfloat16),
            pltpu.VMEM((slots * k_dev, width), jnp.bfloat16),
            pltpu.VMEM((slots * k_dev, 2 * width), jnp.bfloat16),
            pltpu.VMEM((2, slots // CHUNK_TILES, rows_block, chunk), jnp.float32),
            pltpu.VMEM((2, rows_block, 128), jnp.float32),
            pltpu.VMEM((rows_block, 2 * width), jnp.float32),
        ],
        compiler_params=pltpu.CompilerParams(vmem_limit_bytes=48 * 2**20),
        name="attend",
    )(me, ok, first, queries, kv)


def shards(n_pb, n_ka, queries, keys, values, query_pos, key_pos, block_mask):
    q_dev = queries.shape[0]
    k_dev = keys.shape[0]
    n_devices = n_pb * n_ka
    pb, ka = lax.axis_index("pb"), lax.axis_index("ka")
    me = pb * n_ka + ka
    ok = lax.dynamic_slice_in_dim(block_mask, me, 1, 0).reshape(n_devices)
    first = key_pos.reshape(n_devices, k_dev)[:, 0]
    q_first = lax.dynamic_slice_in_dim(query_pos, me * q_dev, 1, 0)[0]
    kv = jnp.concatenate([keys, values], 1)
    rounds = gather_rounds(n_pb, n_ka)
    kv, steps = gather(kv, rounds, n_devices)
    steps = [(s % n_ka) * n_pb + s // n_ka for s in steps]
    where = jnp.stack([ka * n_pb + pb, q_first]).astype(jnp.int32)
    return attend(queries, kv, where, ok, first, steps, k_dev)


def solution(mesh):
    n_pb, n_ka = mesh.shape["pb"], mesh.shape["ka"]
    return jax.shard_map(
        functools.partial(shards, n_pb, n_ka),
        mesh=mesh,
        in_specs=(
            P(("pb", "ka"), None),
            P(("ka", "pb"), None),
            P(("ka", "pb"), None),
            P(),
            P(),
            P(),
        ),
        out_specs=P(("pb", "ka"), None),
        check_vma=False,
    )
```

```python
import functools
import math

import jax
import jax.numpy as jnp
from jax import lax
from jax.experimental import pallas as pl
from jax.experimental.pallas import tpu as pltpu
from jax.sharding import PartitionSpec as P

NEG = -1e30
NEVER = -(2**30)
VMEM = pl.BlockSpec(memory_space=pltpu.VMEM)
SMEM = pl.BlockSpec(memory_space=pltpu.SMEM)
PARAMS = pltpu.CompilerParams(vmem_limit_bytes=48 * 2**20)


def swap(x, step, n_devices):
    return lax.ppermute(x, ("pb", "ka"), [(i, i ^ step) for i in range(n_devices)])


def step_groups(n_pb, n_ka):
    core = n_ka
    bits = [1 << b for b in range((n_pb * n_ka).bit_length() - 1)]
    bits.remove(core)
    groups = []
    while bits:
        pair, bits = bits[:2], bits[2:]
        groups.insert(0, [pair[0], pair[1], pair[0] ^ pair[1]] if len(pair) == 2 else pair)
    far = [[g[1], g[2], g[0]] if len(g) == 3 else g for g in groups[:-1]]
    return far + groups[-1:], core


def plan_kernel(n_pb, n_ka, tiles, q_pos, k_pos, mask, q_ref, qs_ref, reach_ref):
    q_dev, columns = q_ref.shape
    width = qs_ref.shape[1]
    k_dev = k_pos.shape[0] // len(tiles)
    pb, ka = lax.axis_index("pb"), lax.axis_index("ka")
    me = pb * n_ka + ka
    mine = ka * n_pb + pb
    for h in range(columns // width):
        qs_ref[h * q_dev : (h + 1) * q_dev, :] = q_ref[:, h * width : (h + 1) * width]
    first = q_pos[me * q_dev]
    for row, step in enumerate(tiles):
        tile = mine ^ step
        reach = jnp.where(mask[me, tile] == 1, first - k_pos[tile * k_dev], NEVER)
        reach_ref[row : row + 1, :] = jnp.full((1, reach_ref.shape[1]), reach, jnp.int32)


def plan(queries, query_pos, key_pos, block_mask, n_pb, n_ka, tiles, width):
    q_dev, columns = queries.shape
    return pl.pallas_call(
        functools.partial(plan_kernel, n_pb, n_ka, tiles),
        out_shape=(
            jax.ShapeDtypeStruct((q_dev * columns // width, width), queries.dtype),
            jax.ShapeDtypeStruct((len(tiles), 2 * q_dev), jnp.int32),
        ),
        in_specs=[SMEM, SMEM, SMEM, VMEM],
        out_specs=(VMEM, VMEM),
        compiler_params=PARAMS,
        name="plan",
    )(query_pos, key_pos, block_mask, queries)


def part_kernel(rows, q_dev, lanes, has_state, last, *refs):
    refs = list(refs)
    n = len(rows)
    qs_ref, reach_ref = refs[:2]
    pieces, refs = refs[2 : 2 + n], refs[2 + n :]
    if has_state:
        (top_in, acc_in), refs = refs[:2], refs[2:]
    if last:
        out_ref, scores, out_vmem, sems = refs
    else:
        top_out, acc_out, scores = refs
    width = qs_ref.shape[1]
    factor = width ** (-0.5) * math.log2(math.e)
    keys = pieces[0].shape[0]
    blocks = qs_ref.shape[0] // lanes
    pair = reach_ref.shape[1]
    k_dev = keys // (rows[0][1] - rows[0][0])
    ahead = lax.broadcasted_iota(jnp.int32, (k_dev, pair), 0)
    ahead = ahead - lax.broadcasted_iota(jnp.int32, (k_dev, pair), 1) % q_dev
    ones = jnp.ones((16, keys), jnp.bfloat16)
    turned = [jnp.concatenate([piece[:, width:].T, ones], 0) for piece in pieces]

    def score(block, j, q):
        s = lax.dot_general(
            pieces[j][:, :width], q, (((1,), (1,)), ((), ())), preferred_element_type=jnp.float32
        )
        top = None
        for i, row in enumerate(range(*rows[j])):
            allowed = ahead <= reach_ref[row : row + 1, :]
            allowed = jnp.concatenate([allowed] * (lanes // pair), 1)
            tile = jnp.where(allowed, s[i * k_dev : (i + 1) * k_dev], NEG)
            scores[block % 2, j, i * k_dev : (i + 1) * k_dev, :] = tile
            high = jnp.max(tile.reshape(k_dev // 8, 8, lanes), axis=0)
            top = high if top is None else jnp.maximum(top, high)
        return top

    def queries_of(block):
        return qs_ref[block * lanes : (block + 1) * lanes, :]

    def score_all(block):
        q = queries_of(block)
        return functools.reduce(jnp.maximum, [score(block, j, q) for j in range(n)])

    high = score_all(0)
    copies = []
    for block in range(blocks):
        columns = slice(block * lanes, (block + 1) * lanes)
        top = jnp.max(high, axis=0, keepdims=True)
        if has_state:
            old = top_in[:1, columns]
            top = jnp.maximum(top, old)
        high = acc = None
        for j in range(n):
            if block + 1 < blocks:
                more = score(block + 1, j, queries_of(block + 1))
                high = more if high is None else jnp.maximum(high, more)
            p = jnp.exp2((scores[block % 2, j] - top) * factor)
            coarse = p.astype(jnp.bfloat16)
            fine = (p - coarse.astype(jnp.float32)).astype(jnp.bfloat16)
            more = jnp.dot(turned[j], coarse, preferred_element_type=jnp.float32)
            more += jnp.dot(turned[j], fine, preferred_element_type=jnp.float32)
            acc = more if acc is None else acc + more
        if has_state:
            acc = acc + acc_in[:, columns] * jnp.exp2((old - top) * factor)
        if not last:
            top_out[:, columns] = jnp.broadcast_to(top, (8, lanes))
            acc_out[:, columns] = acc
            continue
        result = (acc[:width] * (1.0 / acc[width : width + 1])).astype(jnp.bfloat16).T
        heads = lanes // q_dev
        for i in range(heads):
            h = block * heads + i
            out_vmem[:, h * width : (h + 1) * width] = result[i * q_dev : (i + 1) * q_dev]
        where = (slice(None), slice(block * heads * width, (block + 1) * heads * width))
        copy = pltpu.make_async_copy(out_vmem.at[where], out_ref.at[where], sems.at[block])
        copy.start()
        copies.append(copy)
    for copy in copies:
        copy.wait()


def part(qs, reach, pieces, rows, q_dev, state=None, last=False):
    total, width = qs.shape
    lanes = 4 * q_dev
    keys = pieces[0].shape[0]
    scores = pltpu.VMEM((2, len(pieces), keys, lanes), jnp.float32)
    if last:
        shape = (q_dev, total // q_dev * width)
        out_shape, out_specs = jax.ShapeDtypeStruct(shape, jnp.bfloat16), pl.BlockSpec(memory_space=pl.ANY)
        scratch = [
            scores,
            pltpu.VMEM(shape, jnp.bfloat16),
            pltpu.SemaphoreType.DMA((total // lanes,)),
        ]
    else:
        out_shape = (
            jax.ShapeDtypeStruct((8, total), jnp.float32),
            jax.ShapeDtypeStruct((width + 16, total), jnp.float32),
        )
        out_specs = (VMEM, VMEM)
        scratch = [scores]
    args = [qs, reach, *pieces, *(state or ())]
    n_keys = keys * len(pieces)
    return pl.pallas_call(
        functools.partial(part_kernel, rows, q_dev, lanes, state is not None, last),
        out_shape=out_shape,
        in_specs=[VMEM] * len(args),
        out_specs=out_specs,
        scratch_shapes=scratch,
        compiler_params=PARAMS,
        cost_estimate=pl.CostEstimate(
            flops=8 * total * width * n_keys, bytes_accessed=4 * n_keys * width, transcendentals=total * n_keys
        ),
        name="part_last" if last else "part",
    )(*args)


def shards(n_pb, n_ka, queries, keys, values, query_pos, key_pos, block_mask):
    q_dev, width = queries.shape[0], keys.shape[1]
    n_devices = n_pb * n_ka
    groups, core = step_groups(n_pb, n_ka)

    def send(x, step):
        return swap(x, step, n_devices)

    x, steps = jnp.concatenate([keys, values], 1), [0]
    for group in groups[:-1]:
        x = jnp.concatenate([x] + [send(x, step) for step in group], 0)
        steps = [s ^ g for g in [0] + group for s in steps]
    n = len(steps)
    last = [0] + groups[-1]
    steps = [s ^ g ^ c for c in (0, core) for g in last for s in steps]
    tiles = [(s % n_ka) * n_pb + s // n_ka for s in steps]
    qs, reach = plan(queries, query_pos, key_pos, block_mask, n_pb, n_ka, tiles, width)
    x, qs, reach = lax.optimization_barrier((x, qs, reach))

    mine = [x] + [send(x, step) for step in groups[-1]]
    m = len(mine)
    rows = [(j * n, (j + 1) * n) for j in range(2 * m)]

    def add(state, some, last=False):
        pieces = [piece for piece, _ in some]
        return part(qs, reach, pieces, [rows[j] for _, j in some], q_dev, state, last)

    def after(arrays, state):
        return lax.optimization_barrier((arrays, state))

    state = add(None, [(x, 0), (send(x, core), m)])
    near, late = mine[1:-1], mine[-1]
    if near:
        near, state = after(near, state)
        others = [send(y, core) for y in near]
        state = add(state, [(y, 1 + j) for j, y in enumerate(near)])
    late, state = after(late, state)
    other = send(late, core)
    if near:
        state = add(state, [(y, m + 1 + j) for j, y in enumerate(others)])
    return add(state, [(late, m - 1), (other, 2 * m - 1)], last=True)


def solution(mesh):
    n_pb, n_ka = mesh.shape["pb"], mesh.shape["ka"]
    return jax.shard_map(
        functools.partial(shards, n_pb, n_ka),
        mesh=mesh,
        in_specs=(
            P(("pb", "ka"), None),
            P(("ka", "pb"), None),
            P(("ka", "pb"), None),
            P(),
            P(),
            P(),
        ),
        out_specs=P(("pb", "ka"), None),
        check_vma=False,
    )
```

```python
import functools
import math

import jax
import jax.numpy as jnp
from jax import lax
from jax.experimental import pallas as pl
from jax.experimental.pallas import tpu as pltpu
from jax.sharding import PartitionSpec as P

NEG = -1e30
NEVER = -(2**30)
VMEM = pl.BlockSpec(memory_space=pltpu.VMEM)
SMEM = pl.BlockSpec(memory_space=pltpu.SMEM)
PARAMS = pltpu.CompilerParams(vmem_limit_bytes=48 * 2**20)


def swap(x, step, n_devices):
    return lax.ppermute(x, ("pb", "ka"), [(i, i ^ step) for i in range(n_devices)])


def step_groups(n_pb, n_ka):
    core = n_ka
    bits = [1 << b for b in range((n_pb * n_ka).bit_length() - 1)]
    bits.remove(core)
    groups = []
    while bits:
        pair, bits = bits[:2], bits[2:]
        groups.insert(0, [pair[0], pair[1], pair[0] ^ pair[1]] if len(pair) == 2 else pair)
    far = [[g[1], g[2], g[0]] if len(g) == 3 else g for g in groups[:-1]]
    return far + groups[-1:], core


def plan_kernel(n_pb, n_ka, tiles, q_pos, k_pos, mask, q_ref, qs_ref, reach_ref):
    q_dev, columns = q_ref.shape
    width = qs_ref.shape[1]
    k_dev = k_pos.shape[0] // len(tiles)
    pb, ka = lax.axis_index("pb"), lax.axis_index("ka")
    me = pb * n_ka + ka
    mine = ka * n_pb + pb
    for h in range(columns // width):
        qs_ref[h * q_dev : (h + 1) * q_dev, :] = q_ref[:, h * width : (h + 1) * width]
    first = q_pos[me * q_dev]
    for row, step in enumerate(tiles):
        tile = mine ^ step
        reach = jnp.where(mask[me, tile] == 1, first - k_pos[tile * k_dev], NEVER)
        reach_ref[row : row + 1, :] = jnp.full((1, reach_ref.shape[1]), reach, jnp.int32)


def plan(queries, query_pos, key_pos, block_mask, n_pb, n_ka, tiles, width):
    q_dev, columns = queries.shape
    return pl.pallas_call(
        functools.partial(plan_kernel, n_pb, n_ka, tiles),
        out_shape=(
            jax.ShapeDtypeStruct((q_dev * columns // width, width), queries.dtype),
            jax.ShapeDtypeStruct((len(tiles), 2 * q_dev), jnp.int32),
        ),
        in_specs=[SMEM, SMEM, SMEM, VMEM],
        out_specs=(VMEM, VMEM),
        compiler_params=PARAMS,
        name="plan",
    )(query_pos, key_pos, block_mask, queries)


def part_kernel(rows, q_dev, lanes, has_state, last, *refs):
    refs = list(refs)
    n = len(rows)
    qs_ref, reach_ref = refs[:2]
    pieces, refs = refs[2 : 2 + n], refs[2 + n :]
    if has_state:
        (top_in, acc_in), refs = refs[:2], refs[2:]
    if last:
        out_ref, scores, out_vmem, sems = refs
    else:
        top_out, acc_out, scores = refs
    width = qs_ref.shape[1]
    factor = width ** (-0.5) * math.log2(math.e)
    keys = pieces[0].shape[0]
    blocks = qs_ref.shape[0] // lanes
    pair = reach_ref.shape[1]
    k_dev = keys // (rows[0][1] - rows[0][0])
    ahead = lax.broadcasted_iota(jnp.int32, (k_dev, pair), 0)
    ahead = ahead - lax.broadcasted_iota(jnp.int32, (k_dev, pair), 1) % q_dev
    ones = jnp.ones((16, keys), jnp.bfloat16)
    turned = [jnp.concatenate([piece[:, width:].T, ones], 0) for piece in pieces]

    def score(block, j, q):
        s = lax.dot_general(
            pieces[j][:, :width], q, (((1,), (1,)), ((), ())), preferred_element_type=jnp.float32
        )
        top = None
        for i, row in enumerate(range(*rows[j])):
            allowed = ahead <= reach_ref[row : row + 1, :]
            allowed = jnp.concatenate([allowed] * (lanes // pair), 1)
            tile = jnp.where(allowed, s[i * k_dev : (i + 1) * k_dev], NEG)
            scores[block, j, i * k_dev : (i + 1) * k_dev, :] = tile
            high = jnp.max(tile.reshape(k_dev // 8, 8, lanes), axis=0)
            top = high if top is None else jnp.maximum(top, high)
        return top

    def score_all(block):
        q = qs_ref[block * lanes : (block + 1) * lanes, :]
        return functools.reduce(jnp.maximum, [score(block, j, q) for j in range(n)])

    highs = [score_all(block) for block in range(blocks)]
    copies = []
    for block in range(blocks):
        columns = slice(block * lanes, (block + 1) * lanes)
        top = jnp.max(highs[block], axis=0, keepdims=True)
        if has_state:
            old = top_in[:1, columns]
            top = jnp.maximum(top, old)
        acc = None
        for j in range(n):
            p = jnp.exp2((scores[block, j] - top) * factor)
            coarse = p.astype(jnp.bfloat16)
            fine = (p - coarse.astype(jnp.float32)).astype(jnp.bfloat16)
            more = jnp.dot(turned[j], coarse, preferred_element_type=jnp.float32)
            more += jnp.dot(turned[j], fine, preferred_element_type=jnp.float32)
            acc = more if acc is None else acc + more
        if has_state:
            acc = acc + acc_in[:, columns] * jnp.exp2((old - top) * factor)
        if not last:
            top_out[:, columns] = jnp.broadcast_to(top, (8, lanes))
            acc_out[:, columns] = acc
            continue
        result = (acc[:width] * (1.0 / acc[width : width + 1])).astype(jnp.bfloat16).T
        heads = lanes // q_dev
        for i in range(heads):
            h = block * heads + i
            out_vmem[:, h * width : (h + 1) * width] = result[i * q_dev : (i + 1) * q_dev]
        where = (slice(None), slice(block * heads * width, (block + 1) * heads * width))
        copy = pltpu.make_async_copy(out_vmem.at[where], out_ref.at[where], sems.at[block])
        copy.start()
        copies.append(copy)
    for copy in copies:
        copy.wait()


def part(qs, reach, pieces, rows, q_dev, state=None, last=False):
    total, width = qs.shape
    lanes = 4 * q_dev
    keys = pieces[0].shape[0]
    scores = pltpu.VMEM((total // lanes, len(pieces), keys, lanes), jnp.float32)
    if last:
        shape = (q_dev, total // q_dev * width)
        out_shape, out_specs = jax.ShapeDtypeStruct(shape, jnp.bfloat16), pl.BlockSpec(memory_space=pl.ANY)
        scratch = [
            scores,
            pltpu.VMEM(shape, jnp.bfloat16),
            pltpu.SemaphoreType.DMA((total // lanes,)),
        ]
    else:
        out_shape = (
            jax.ShapeDtypeStruct((8, total), jnp.float32),
            jax.ShapeDtypeStruct((width + 16, total), jnp.float32),
        )
        out_specs = (VMEM, VMEM)
        scratch = [scores]
    args = [qs, reach, *pieces, *(state or ())]
    n_keys = keys * len(pieces)
    return pl.pallas_call(
        functools.partial(part_kernel, rows, q_dev, lanes, state is not None, last),
        out_shape=out_shape,
        in_specs=[VMEM] * len(args),
        out_specs=out_specs,
        scratch_shapes=scratch,
        compiler_params=PARAMS,
        cost_estimate=pl.CostEstimate(
            flops=8 * total * width * n_keys, bytes_accessed=4 * n_keys * width, transcendentals=total * n_keys
        ),
        name="part_last" if last else "part",
    )(*args)


def shards(n_pb, n_ka, queries, keys, values, query_pos, key_pos, block_mask):
    q_dev, width = queries.shape[0], keys.shape[1]
    n_devices = n_pb * n_ka
    groups, core = step_groups(n_pb, n_ka)

    def send(x, step):
        return swap(x, step, n_devices)

    x, steps = jnp.concatenate([keys, values], 1), [0]
    for group in groups[:-1]:
        x = jnp.concatenate([x] + [send(x, step) for step in group], 0)
        steps = [s ^ g for g in [0] + group for s in steps]
    n = len(steps)
    last = [0] + groups[-1]
    steps = [s ^ g ^ c for c in (0, core) for g in last for s in steps]
    tiles = [(s % n_ka) * n_pb + s // n_ka for s in steps]
    qs, reach = plan(queries, query_pos, key_pos, block_mask, n_pb, n_ka, tiles, width)
    x, qs, reach = lax.optimization_barrier((x, qs, reach))

    mine = [x] + [send(x, step) for step in groups[-1]]
    m = len(mine)
    rows = [(j * n, (j + 1) * n) for j in range(2 * m)]

    def add(state, some, last=False):
        pieces = [piece for piece, _ in some]
        return part(qs, reach, pieces, [rows[j] for _, j in some], q_dev, state, last)

    def after(arrays, state):
        return lax.optimization_barrier((arrays, state))

    state = add(None, [(x, 0)])
    near, late = mine[1:-1], mine[-1]
    if near:
        near[0], state = after(near[0], state)
    others = [send(y, core) for y in near]
    other = send(x, core)
    if near:
        state = add(state, [(y, 1 + j) for j, y in enumerate(near)])
    late, state = after(late, state)
    last = send(late, core)
    some = [(other, m)] + [(y, m + 1 + j) for j, y in enumerate(others)] + [(late, m - 1)]
    state = add(state, some)
    return add(state, [(last, 2 * m - 1)], last=True)


def solution(mesh):
    n_pb, n_ka = mesh.shape["pb"], mesh.shape["ka"]
    return jax.shard_map(
        functools.partial(shards, n_pb, n_ka),
        mesh=mesh,
        in_specs=(
            P(("pb", "ka"), None),
            P(("ka", "pb"), None),
            P(("ka", "pb"), None),
            P(),
            P(),
            P(),
        ),
        out_specs=P(("pb", "ka"), None),
        check_vma=False,
    )
```

```python
import functools
import math

import jax
import jax.numpy as jnp
from jax import lax
from jax.experimental import pallas as pl
from jax.experimental.pallas import tpu as pltpu
from jax.sharding import PartitionSpec as P

NEG = -1e30
NEVER = -(2**30)
VMEM = pl.BlockSpec(memory_space=pltpu.VMEM)
SMEM = pl.BlockSpec(memory_space=pltpu.SMEM)
PARAMS = pltpu.CompilerParams(vmem_limit_bytes=48 * 2**20)


def swap(x, step, n_devices):
    return lax.ppermute(x, ("pb", "ka"), [(i, i ^ step) for i in range(n_devices)])


def step_groups(n_pb, n_ka):
    core = n_ka
    bits = [1 << b for b in range((n_pb * n_ka).bit_length() - 1)]
    bits.remove(core)
    groups = []
    while bits:
        pair, bits = bits[:2], bits[2:]
        groups.insert(0, [pair[0], pair[1], pair[0] ^ pair[1]] if len(pair) == 2 else pair)
    far = [[g[1], g[2], g[0]] if len(g) == 3 else g for g in groups[:-1]]
    near = [[g[0], g[2], g[1]] if len(g) == 3 else g for g in groups[-1:]]
    return far + near, core


def plan_kernel(n_pb, n_ka, tiles, q_pos, k_pos, mask, q_ref, qs_ref, reach_ref):
    q_dev, columns = q_ref.shape
    width = qs_ref.shape[1]
    k_dev = k_pos.shape[0] // len(tiles)
    pb, ka = lax.axis_index("pb"), lax.axis_index("ka")
    me = pb * n_ka + ka
    mine = ka * n_pb + pb
    for h in range(columns // width):
        qs_ref[h * q_dev : (h + 1) * q_dev, :] = q_ref[:, h * width : (h + 1) * width]
    first = q_pos[me * q_dev]
    for row, step in enumerate(tiles):
        tile = mine ^ step
        reach = jnp.where(mask[me, tile] == 1, first - k_pos[tile * k_dev], NEVER)
        reach_ref[row : row + 1, :] = jnp.full((1, reach_ref.shape[1]), reach, jnp.int32)


def plan(queries, query_pos, key_pos, block_mask, n_pb, n_ka, tiles, width):
    q_dev, columns = queries.shape
    return pl.pallas_call(
        functools.partial(plan_kernel, n_pb, n_ka, tiles),
        out_shape=(
            jax.ShapeDtypeStruct((q_dev * columns // width, width), queries.dtype),
            jax.ShapeDtypeStruct((len(tiles), 2 * q_dev), jnp.int32),
        ),
        in_specs=[SMEM, SMEM, SMEM, VMEM],
        out_specs=(VMEM, VMEM),
        compiler_params=PARAMS,
        name="plan",
    )(query_pos, key_pos, block_mask, queries)


def part_kernel(rows, q_dev, lanes, has_state, last, pack, *refs):
    refs = list(refs)
    n = len(rows)
    qs_ref, reach_ref = refs[:2]
    pieces, refs = refs[2 : 2 + n], refs[2 + n :]
    if has_state:
        (top_in, acc_in), refs = refs[:2], refs[2:]
    if last:
        (out_ref, out_vmem, sems), refs = refs[:3], refs[3:]
    else:
        (top_out, acc_out), refs = refs[:2], refs[2:]
    scores = refs[0]
    width = qs_ref.shape[1]
    factor = width ** (-0.5) * math.log2(math.e)
    keys = pieces[0].shape[0]
    per_piece = rows[0][1] - rows[0][0]
    blocks = qs_ref.shape[0] // lanes
    pair = reach_ref.shape[1]
    k_dev = keys // per_piece

    def attend(pieces, reach_ref, rows):
        ahead = lax.broadcasted_iota(jnp.int32, (k_dev, pair), 0)
        ahead = ahead - lax.broadcasted_iota(jnp.int32, (k_dev, pair), 1) % q_dev
        ones = jnp.ones((16, keys), jnp.bfloat16)
        turned = [jnp.concatenate([piece[:, width:].T, ones], 0) for piece in pieces]

        def score(block, j, q):
            s = lax.dot_general(
                pieces[j][:, :width], q, (((1,), (1,)), ((), ())), preferred_element_type=jnp.float32
            )
            top = None
            for i, row in enumerate(range(*rows[j])):
                allowed = ahead <= reach_ref[row : row + 1, :]
                allowed = jnp.concatenate([allowed] * (lanes // pair), 1)
                tile = jnp.where(allowed, s[i * k_dev : (i + 1) * k_dev], NEG)
                scores[block, j, i * k_dev : (i + 1) * k_dev, :] = tile
                high = jnp.max(tile.reshape(k_dev // 8, 8, lanes), axis=0)
                top = high if top is None else jnp.maximum(top, high)
            return top

        def score_all(block):
            q = qs_ref[block * lanes : (block + 1) * lanes, :]
            return [score(block, j, q) for j in range(len(pieces))]

        highs = [score_all(block) for block in range(blocks)]
        copies = []
        for block in range(blocks):
            columns = slice(block * lanes, (block + 1) * lanes)
            tops = [jnp.max(high, axis=0, keepdims=True) for high in highs[block]]
            if has_state:
                old = top_in[:1, columns]
                tops.append(old)
            top = functools.reduce(jnp.maximum, tops)
            acc = None
            for j in range(len(pieces)):
                p = jnp.exp2((scores[block, j] - top) * factor)
                coarse = p.astype(jnp.bfloat16)
                fine = (p - coarse.astype(jnp.float32)).astype(jnp.bfloat16)
                more = jnp.dot(turned[j], coarse, preferred_element_type=jnp.float32)
                more += jnp.dot(turned[j], fine, preferred_element_type=jnp.float32)
                acc = more if acc is None else acc + more
            if has_state:
                before = acc_in[:, columns] * jnp.exp2((old - top) * factor)
                acc = before if acc is None else acc + before
            if not last:
                top_out[:, columns] = jnp.broadcast_to(top, (8, lanes))
                acc_out[:, columns] = acc
                continue
            result = (acc[:width] * (1.0 / acc[width : width + 1])).astype(jnp.bfloat16).T
            heads = lanes // q_dev
            for i in range(heads):
                h = block * heads + i
                out_vmem[:, h * width : (h + 1) * width] = result[i * q_dev : (i + 1) * q_dev]
            where = (slice(None), slice(block * heads * width, (block + 1) * heads * width))
            copy = pltpu.make_async_copy(out_vmem.at[where], out_ref.at[where], sems.at[block])
            copy.start()
            copies.append(copy)
        for copy in copies:
            copy.wait()

    if not pack:
        attend(pieces, reach_ref, rows)
        return

    packed, packed_reach = refs[1:]
    packed[...] = jnp.zeros_like(packed)
    packed_reach[...] = jnp.full_like(packed_reach, NEVER)
    at = None
    for piece, (low, high) in zip(pieces, rows):
        for i, row in enumerate(range(low, high)):
            to_rows, to_row = slice(0, k_dev), slice(0, 1)
            if at is not None:
                to_rows, to_row = pl.ds(pl.multiple_of(at * k_dev, k_dev), k_dev), pl.ds(at, 1)
            packed[to_rows, :] = piece[i * k_dev : (i + 1) * k_dev, :]
            packed_reach[to_row, :] = reach_ref[row : row + 1, :]
            more = jnp.where(reach_ref[row, 0] > -k_dev, 1, 0)
            at = more if at is None else at + more
    used = (at + per_piece - 1) // per_piece
    for count in range(n + 1):

        @pl.when(used == count)
        def _():
            some = [packed.at[pl.ds(j * keys, keys), :] for j in range(count)]
            attend(some, packed_reach, [(j * per_piece, (j + 1) * per_piece) for j in range(count)])


def part(qs, reach, pieces, rows, q_dev, state=None, last=False):
    total, width = qs.shape
    lanes = 4 * q_dev
    keys, columns = pieces[0].shape
    n = len(pieces)
    pack = state is not None and n > 1
    scratch = [pltpu.VMEM((total // lanes, n, keys, lanes), jnp.float32)]
    if pack:
        slots = n * (rows[0][1] - rows[0][0])
        scratch += [
            pltpu.VMEM((n * keys, columns), jnp.bfloat16),
            pltpu.VMEM((slots, reach.shape[1]), jnp.int32),
        ]
    if last:
        shape = (q_dev, total // q_dev * width)
        out_shape, out_specs = jax.ShapeDtypeStruct(shape, jnp.bfloat16), pl.BlockSpec(memory_space=pl.ANY)
        scratch = [pltpu.VMEM(shape, jnp.bfloat16), pltpu.SemaphoreType.DMA((total // lanes,))] + scratch
    else:
        out_shape = (
            jax.ShapeDtypeStruct((8, total), jnp.float32),
            jax.ShapeDtypeStruct((width + 16, total), jnp.float32),
        )
        out_specs = (VMEM, VMEM)
    args = [qs, reach, *pieces, *(state or ())]
    n_keys = keys * n
    return pl.pallas_call(
        functools.partial(part_kernel, rows, q_dev, lanes, state is not None, last, pack),
        out_shape=out_shape,
        in_specs=[VMEM] * len(args),
        out_specs=out_specs,
        scratch_shapes=scratch,
        compiler_params=PARAMS,
        cost_estimate=pl.CostEstimate(
            flops=8 * total * width * n_keys, bytes_accessed=4 * n_keys * width, transcendentals=total * n_keys
        ),
        name="part_last" if last else "part",
    )(*args)


def shards(n_pb, n_ka, queries, keys, values, query_pos, key_pos, block_mask):
    q_dev, width = queries.shape[0], keys.shape[1]
    n_devices = n_pb * n_ka
    groups, core = step_groups(n_pb, n_ka)

    def send(x, step):
        return swap(x, step, n_devices)

    x, steps = jnp.concatenate([keys, values], 1), [0]
    for group in groups[:-1]:
        x = jnp.concatenate([x] + [send(x, step) for step in group], 0)
        steps = [s ^ g for g in [0] + group for s in steps]
    n = len(steps)
    last = [0] + groups[-1]
    steps = [s ^ g ^ c for c in (0, core) for g in last for s in steps]
    tiles = [(s % n_ka) * n_pb + s // n_ka for s in steps]
    qs, reach = plan(queries, query_pos, key_pos, block_mask, n_pb, n_ka, tiles, width)
    x, qs, reach = lax.optimization_barrier((x, qs, reach))

    mine = [x] + [send(x, step) for step in groups[-1]]
    m = len(mine)
    rows = [(j * n, (j + 1) * n) for j in range(2 * m)]

    def add(state, some, last=False):
        pieces = [piece for piece, _ in some]
        return part(qs, reach, pieces, [rows[j] for _, j in some], q_dev, state, last)

    def after(arrays, state):
        return lax.optimization_barrier((arrays, state))

    state = add(None, [(x, 0)])
    some = []
    if m > 2:
        mine[1], state = after(mine[1], state)
        some = [(send(mine[1], core), m + 1)]
    some = [(send(x, core), m)] + some
    if m > 2:
        state = add(state, [(mine[1], 1)])
    k = min(2, m - 1)
    rest, state = after(mine[k:], state)
    others = [send(y, core) for y in rest]
    state = add(state, some + [(y, k + j) for j, y in enumerate(rest)])
    return add(state, [(y, m + k + j) for j, y in enumerate(others)], last=True)


def solution(mesh):
    n_pb, n_ka = mesh.shape["pb"], mesh.shape["ka"]
    return jax.shard_map(
        functools.partial(shards, n_pb, n_ka),
        mesh=mesh,
        in_specs=(
            P(("pb", "ka"), None),
            P(("ka", "pb"), None),
            P(("ka", "pb"), None),
            P(),
            P(),
            P(),
        ),
        out_specs=P(("pb", "ka"), None),
        check_vma=False,
    )
```

```python
import functools
import math

import jax
import jax.numpy as jnp
from jax import lax
from jax.experimental import pallas as pl
from jax.experimental.pallas import tpu as pltpu
from jax.sharding import PartitionSpec as P

NEG = -1e30
NEVER = -(2**30)
VMEM = pl.BlockSpec(memory_space=pltpu.VMEM)
SMEM = pl.BlockSpec(memory_space=pltpu.SMEM)
PARAMS = pltpu.CompilerParams(vmem_limit_bytes=48 * 2**20)


def swap(x, step, n_devices):
    return lax.ppermute(x, ("pb", "ka"), [(i, i ^ step) for i in range(n_devices)])


def step_groups(n_pb, n_ka):
    core = n_ka
    bits = [1 << b for b in range((n_pb * n_ka).bit_length() - 1)]
    bits.remove(core)
    groups = []
    while bits:
        pair, bits = bits[:2], bits[2:]
        groups.insert(0, [pair[0], pair[1], pair[0] ^ pair[1]] if len(pair) == 2 else pair)
    far = [[g[1], g[2], g[0]] if len(g) == 3 else g for g in groups[:-1]]
    near = [[g[0], g[2], g[1]] if len(g) == 3 else g for g in groups[-1:]]
    return far + near, core


def plan_kernel(n_pb, n_ka, tiles, q_pos, k_pos, mask, q_ref, qs_ref, reach_ref):
    q_dev, columns = q_ref.shape
    width = qs_ref.shape[1]
    k_dev = k_pos.shape[0] // len(tiles)
    pb, ka = lax.axis_index("pb"), lax.axis_index("ka")
    me = pb * n_ka + ka
    mine = ka * n_pb + pb
    for h in range(columns // width):
        qs_ref[h * q_dev : (h + 1) * q_dev, :] = q_ref[:, h * width : (h + 1) * width]
    first = q_pos[me * q_dev]
    for row, step in enumerate(tiles):
        tile = mine ^ step
        reach = jnp.where(mask[me, tile] == 1, first - k_pos[tile * k_dev], NEVER)
        reach_ref[row : row + 1, :] = jnp.full((1, reach_ref.shape[1]), reach, jnp.int32)


def plan(queries, query_pos, key_pos, block_mask, n_pb, n_ka, tiles, width):
    q_dev, columns = queries.shape
    return pl.pallas_call(
        functools.partial(plan_kernel, n_pb, n_ka, tiles),
        out_shape=(
            jax.ShapeDtypeStruct((q_dev * columns // width, width), queries.dtype),
            jax.ShapeDtypeStruct((len(tiles), 2 * q_dev), jnp.int32),
        ),
        in_specs=[SMEM, SMEM, SMEM, VMEM],
        out_specs=(VMEM, VMEM),
        compiler_params=PARAMS,
        name="plan",
    )(query_pos, key_pos, block_mask, queries)


def part_kernel(rows, q_dev, lanes, has_state, last, pack, *refs):
    refs = list(refs)
    n = len(rows)
    qs_ref, reach_ref = refs[:2]
    pieces, refs = refs[2 : 2 + n], refs[2 + n :]
    if has_state:
        (top_in, acc_in), refs = refs[:2], refs[2:]
    if last:
        (out_ref, out_vmem, sems), refs = refs[:3], refs[3:]
    else:
        (top_out, acc_out), refs = refs[:2], refs[2:]
    scores = refs[0]
    width = qs_ref.shape[1]
    factor = width ** (-0.5) * math.log2(math.e)
    keys = pieces[0].shape[0]
    per_piece = rows[0][1] - rows[0][0]
    blocks = qs_ref.shape[0] // lanes
    pair = reach_ref.shape[1]
    k_dev = keys // per_piece

    def attend(pieces, reach_ref, rows):
        ahead = lax.broadcasted_iota(jnp.int32, (k_dev, pair), 0)
        ahead = ahead - lax.broadcasted_iota(jnp.int32, (k_dev, pair), 1) % q_dev
        ones = jnp.ones((16, keys), jnp.bfloat16)
        turned = [jnp.concatenate([piece[:, width:].T, ones], 0) for piece in pieces]

        def score(block, j, q):
            s = lax.dot_general(
                pieces[j][:, :width], q, (((1,), (1,)), ((), ())), preferred_element_type=jnp.float32
            )
            top = None
            for i, row in enumerate(range(*rows[j])):
                allowed = ahead <= reach_ref[row : row + 1, :]
                allowed = jnp.concatenate([allowed] * (lanes // pair), 1)
                tile = jnp.where(allowed, s[i * k_dev : (i + 1) * k_dev], NEG)
                scores[block, j, i * k_dev : (i + 1) * k_dev, :] = tile
                high = jnp.max(tile.reshape(k_dev // 8, 8, lanes), axis=0)
                top = high if top is None else jnp.maximum(top, high)
            return top

        def score_all(block):
            q = qs_ref[block * lanes : (block + 1) * lanes, :]
            return [score(block, j, q) for j in range(len(pieces))]

        highs = [score_all(block) for block in range(blocks)]
        copies = []
        for block in range(blocks):
            columns = slice(block * lanes, (block + 1) * lanes)
            tops = [jnp.max(high, axis=0, keepdims=True) for high in highs[block]]
            if has_state:
                old = top_in[:1, columns]
                tops.append(old)
            top = functools.reduce(jnp.maximum, tops)
            acc = None
            for j in range(len(pieces)):
                p = jnp.exp2((scores[block, j] - top) * factor)
                coarse = p.astype(jnp.bfloat16)
                fine = (p - coarse.astype(jnp.float32)).astype(jnp.bfloat16)
                more = jnp.dot(turned[j], coarse, preferred_element_type=jnp.float32)
                more += jnp.dot(turned[j], fine, preferred_element_type=jnp.float32)
                acc = more if acc is None else acc + more
            if has_state:
                before = acc_in[:, columns] * jnp.exp2((old - top) * factor)
                acc = before if acc is None else acc + before
            if not last:
                top_out[:, columns] = jnp.broadcast_to(top, (8, lanes))
                acc_out[:, columns] = acc
                continue
            result = (acc[:width] * (1.0 / acc[width : width + 1])).astype(jnp.bfloat16).T
            heads = lanes // q_dev
            for i in range(heads):
                h = block * heads + i
                out_vmem[:, h * width : (h + 1) * width] = result[i * q_dev : (i + 1) * q_dev]
            where = (slice(None), slice(block * heads * width, (block + 1) * heads * width))
            copy = pltpu.make_async_copy(out_vmem.at[where], out_ref.at[where], sems.at[block])
            copy.start()
            copies.append(copy)
        for copy in copies:
            copy.wait()

    if not pack:
        attend(pieces, reach_ref, rows)
        return

    packed, packed_reach = refs[1:]
    packed[...] = jnp.zeros_like(packed)
    packed_reach[...] = jnp.full_like(packed_reach, NEVER)
    at = None
    for piece, (low, high) in zip(pieces, rows):
        for i, row in enumerate(range(low, high)):
            to_rows, to_row = slice(0, k_dev), slice(0, 1)
            if at is not None:
                to_rows, to_row = pl.ds(pl.multiple_of(at * k_dev, k_dev), k_dev), pl.ds(at, 1)
            packed[to_rows, :] = piece[i * k_dev : (i + 1) * k_dev, :]
            packed_reach[to_row, :] = reach_ref[row : row + 1, :]
            more = jnp.where(reach_ref[row, 0] > -k_dev, 1, 0)
            at = more if at is None else at + more
    used = (at + per_piece - 1) // per_piece
    for count in range(n + 1):

        @pl.when(used == count)
        def _():
            some = [packed.at[pl.ds(j * keys, keys), :] for j in range(count)]
            attend(some, packed_reach, [(j * per_piece, (j + 1) * per_piece) for j in range(count)])


def part(qs, reach, pieces, rows, q_dev, state=None, last=False):
    total, width = qs.shape
    lanes = 4 * q_dev
    keys, columns = pieces[0].shape
    n = len(pieces)
    pack = state is not None and n > 1
    scratch = [pltpu.VMEM((total // lanes, n, keys, lanes), jnp.float32)]
    if pack:
        slots = n * (rows[0][1] - rows[0][0])
        scratch += [
            pltpu.VMEM((n * keys, columns), jnp.bfloat16),
            pltpu.VMEM((slots, reach.shape[1]), jnp.int32),
        ]
    if last:
        shape = (q_dev, total // q_dev * width)
        out_shape, out_specs = jax.ShapeDtypeStruct(shape, jnp.bfloat16), pl.BlockSpec(memory_space=pl.ANY)
        scratch = [pltpu.VMEM(shape, jnp.bfloat16), pltpu.SemaphoreType.DMA((total // lanes,))] + scratch
    else:
        out_shape = (
            jax.ShapeDtypeStruct((8, total), jnp.float32),
            jax.ShapeDtypeStruct((width + 16, total), jnp.float32),
        )
        out_specs = (VMEM, VMEM)
    args = [qs, reach, *pieces, *(state or ())]
    n_keys = keys * n
    return pl.pallas_call(
        functools.partial(part_kernel, rows, q_dev, lanes, state is not None, last, pack),
        out_shape=out_shape,
        in_specs=[VMEM] * len(args),
        out_specs=out_specs,
        scratch_shapes=scratch,
        compiler_params=PARAMS,
        cost_estimate=pl.CostEstimate(
            flops=8 * total * width * n_keys, bytes_accessed=4 * n_keys * width, transcendentals=total * n_keys
        ),
        name="part_last" if last else "part",
    )(*args)


def shards(n_pb, n_ka, queries, keys, values, query_pos, key_pos, block_mask):
    q_dev, width = queries.shape[0], keys.shape[1]
    n_devices = n_pb * n_ka
    groups, core = step_groups(n_pb, n_ka)

    def send(x, step):
        return swap(x, step, n_devices)

    x, steps = jnp.concatenate([keys, values], 1), [0]
    for group in groups[:-1]:
        x = jnp.concatenate([x] + [send(x, step) for step in group], 0)
        steps = [s ^ g for g in [0] + group for s in steps]
    n = len(steps)
    last = [0] + groups[-1]
    steps = [s ^ g ^ c for c in (0, core) for g in last for s in steps]
    tiles = [(s % n_ka) * n_pb + s // n_ka for s in steps]
    qs, reach = plan(queries, query_pos, key_pos, block_mask, n_pb, n_ka, tiles, width)
    x, qs, reach = lax.optimization_barrier((x, qs, reach))

    mine = [x] + [send(x, step) for step in groups[-1]]
    m = len(mine)
    rows = [(j * n, (j + 1) * n) for j in range(2 * m)]

    def add(state, some, last=False):
        pieces = [piece for piece, _ in some]
        return part(qs, reach, pieces, [rows[j] for _, j in some], q_dev, state, last)

    def after(arrays, state):
        return lax.optimization_barrier((arrays, state))

    state = add(None, [(x, 0)])
    some = []
    if m > 2:
        mine[1], state = after(mine[1], state)
        some = [(send(mine[1], core), m + 1)]
    some = [(send(x, core), m)] + some
    if m > 2:
        state = add(state, [(mine[1], 1)])
    k = min(2, m - 1)
    y, state = after(mine[k], state)
    rest = [y] + mine[k + 1 :]
    others = [send(y, core) for y in rest]
    state = add(state, some + [(y, k + j) for j, y in enumerate(rest)])
    return add(state, [(y, m + k + j) for j, y in enumerate(others)], last=True)


def solution(mesh):
    n_pb, n_ka = mesh.shape["pb"], mesh.shape["ka"]
    return jax.shard_map(
        functools.partial(shards, n_pb, n_ka),
        mesh=mesh,
        in_specs=(
            P(("pb", "ka"), None),
            P(("ka", "pb"), None),
            P(("ka", "pb"), None),
            P(),
            P(),
            P(),
        ),
        out_specs=P(("pb", "ka"), None),
        check_vma=False,
    )
```

```python
import functools
import math

import jax
import jax.numpy as jnp
from jax import lax
from jax.experimental import pallas as pl
from jax.experimental.pallas import tpu as pltpu
from jax.sharding import PartitionSpec as P

NEG = -1e30
NEVER = -(2**30)
VMEM = pl.BlockSpec(memory_space=pltpu.VMEM)
SMEM = pl.BlockSpec(memory_space=pltpu.SMEM)
PARAMS = pltpu.CompilerParams(vmem_limit_bytes=48 * 2**20)


def swap(x, step, n_devices):
    return lax.ppermute(x, ("pb", "ka"), [(i, i ^ step) for i in range(n_devices)])


def step_groups(n_pb, n_ka):
    core = n_ka
    bits = [1 << b for b in range((n_pb * n_ka).bit_length() - 1)]
    bits.remove(core)
    groups = []
    while bits:
        pair, bits = bits[:2], bits[2:]
        groups.insert(0, [pair[0], pair[1], pair[0] ^ pair[1]] if len(pair) == 2 else pair)
    far = [[g[1], g[2], g[0]] if len(g) == 3 else g for g in groups[:-1]]
    near = [[g[0], g[2], g[1]] if len(g) == 3 else g for g in groups[-1:]]
    return far + near, core


def plan_kernel(n_pb, n_ka, tiles, q_pos, k_pos, mask, q_ref, qs_ref, reach_ref):
    q_dev, columns = q_ref.shape
    width = qs_ref.shape[1]
    k_dev = k_pos.shape[0] // len(tiles)
    pb, ka = lax.axis_index("pb"), lax.axis_index("ka")
    me = pb * n_ka + ka
    mine = ka * n_pb + pb
    for h in range(columns // width):
        qs_ref[h * q_dev : (h + 1) * q_dev, :] = q_ref[:, h * width : (h + 1) * width]
    first = q_pos[me * q_dev]
    for row, step in enumerate(tiles):
        tile = mine ^ step
        reach = jnp.where(mask[me, tile] == 1, first - k_pos[tile * k_dev], NEVER)
        reach_ref[row : row + 1, :] = jnp.full((1, reach_ref.shape[1]), reach, jnp.int32)


def plan(queries, query_pos, key_pos, block_mask, n_pb, n_ka, tiles, width):
    q_dev, columns = queries.shape
    return pl.pallas_call(
        functools.partial(plan_kernel, n_pb, n_ka, tiles),
        out_shape=(
            jax.ShapeDtypeStruct((q_dev * columns // width, width), queries.dtype),
            jax.ShapeDtypeStruct((len(tiles), 2 * q_dev), jnp.int32),
        ),
        in_specs=[SMEM, SMEM, SMEM, VMEM],
        out_specs=(VMEM, VMEM),
        compiler_params=PARAMS,
        name="plan",
    )(query_pos, key_pos, block_mask, queries)


def part_kernel(rows, q_dev, lanes, has_state, last, pack, *refs):
    refs = list(refs)
    n = len(rows)
    qs_ref, reach_ref = refs[:2]
    pieces, refs = refs[2 : 2 + n], refs[2 + n :]
    if has_state:
        (top_in, acc_in), refs = refs[:2], refs[2:]
    if last:
        (out_ref, out_vmem, sems), refs = refs[:3], refs[3:]
    else:
        (top_out, acc_out), refs = refs[:2], refs[2:]
    scores = refs[0]
    width = qs_ref.shape[1]
    factor = width ** (-0.5) * math.log2(math.e)
    keys = pieces[0].shape[0]
    per_piece = rows[0][1] - rows[0][0]
    blocks = qs_ref.shape[0] // lanes
    pair = reach_ref.shape[1]
    k_dev = keys // per_piece

    def attend(pieces, reach_ref, rows):
        ahead = lax.broadcasted_iota(jnp.int32, (k_dev, pair), 0)
        ahead = ahead - lax.broadcasted_iota(jnp.int32, (k_dev, pair), 1) % q_dev
        ones = jnp.ones((16, keys), jnp.bfloat16)
        turned = [jnp.concatenate([piece[:, width:].T, ones], 0) for piece in pieces]

        def score(block, j, q):
            s = lax.dot_general(
                pieces[j][:, :width], q, (((1,), (1,)), ((), ())), preferred_element_type=jnp.float32
            )
            top = None
            for i, row in enumerate(range(*rows[j])):
                allowed = ahead <= reach_ref[row : row + 1, :]
                allowed = jnp.concatenate([allowed] * (lanes // pair), 1)
                tile = jnp.where(allowed, s[i * k_dev : (i + 1) * k_dev], NEG)
                scores[block, j, i * k_dev : (i + 1) * k_dev, :] = tile
                high = jnp.max(tile.reshape(k_dev // 8, 8, lanes), axis=0)
                top = high if top is None else jnp.maximum(top, high)
            return top

        def score_all(block):
            q = qs_ref[block * lanes : (block + 1) * lanes, :]
            return [score(block, j, q) for j in range(len(pieces))]

        highs = [score_all(block) for block in range(blocks)]
        copies = []
        for block in range(blocks):
            columns = slice(block * lanes, (block + 1) * lanes)
            tops = [jnp.max(high, axis=0, keepdims=True) for high in highs[block]]
            if has_state:
                old = top_in[:1, columns]
                tops.append(old)
            top = functools.reduce(jnp.maximum, tops)
            acc = None
            for j in range(len(pieces)):
                p = jnp.exp2((scores[block, j] - top) * factor)
                coarse = p.astype(jnp.bfloat16)
                fine = (p - coarse.astype(jnp.float32)).astype(jnp.bfloat16)
                more = jnp.dot(turned[j], coarse, preferred_element_type=jnp.float32)
                more += jnp.dot(turned[j], fine, preferred_element_type=jnp.float32)
                acc = more if acc is None else acc + more
            if has_state:
                before = acc_in[:, columns] * jnp.exp2((old - top) * factor)
                acc = before if acc is None else acc + before
            if not last:
                top_out[:, columns] = jnp.broadcast_to(top, (8, lanes))
                acc_out[:, columns] = acc
                continue
            result = (acc[:width] * (1.0 / acc[width : width + 1])).astype(jnp.bfloat16).T
            heads = lanes // q_dev
            for i in range(heads):
                h = block * heads + i
                out_vmem[:, h * width : (h + 1) * width] = result[i * q_dev : (i + 1) * q_dev]
            where = (slice(None), slice(block * heads * width, (block + 1) * heads * width))
            copy = pltpu.make_async_copy(out_vmem.at[where], out_ref.at[where], sems.at[block])
            copy.start()
            copies.append(copy)
        for copy in copies:
            copy.wait()

    if not pack:
        attend(pieces, reach_ref, rows)
        return

    packed, packed_reach = refs[1:]
    packed[...] = jnp.zeros_like(packed)
    packed_reach[...] = jnp.full_like(packed_reach, NEVER)
    at = None
    for piece, (low, high) in zip(pieces, rows):
        for i, row in enumerate(range(low, high)):
            to_rows, to_row = slice(0, k_dev), slice(0, 1)
            if at is not None:
                to_rows, to_row = pl.ds(pl.multiple_of(at * k_dev, k_dev), k_dev), pl.ds(at, 1)
            packed[to_rows, :] = piece[i * k_dev : (i + 1) * k_dev, :]
            packed_reach[to_row, :] = reach_ref[row : row + 1, :]
            more = jnp.where(reach_ref[row, 0] > -k_dev, 1, 0)
            at = more if at is None else at + more
    used = (at + per_piece - 1) // per_piece
    for count in range(n + 1):

        @pl.when(used == count)
        def _():
            some = [packed.at[pl.ds(j * keys, keys), :] for j in range(count)]
            attend(some, packed_reach, [(j * per_piece, (j + 1) * per_piece) for j in range(count)])


def part(qs, reach, pieces, rows, q_dev, state=None, last=False):
    total, width = qs.shape
    lanes = 4 * q_dev
    keys, columns = pieces[0].shape
    n = len(pieces)
    pack = state is not None and n > 1
    scratch = [pltpu.VMEM((total // lanes, n, keys, lanes), jnp.float32)]
    if pack:
        slots = n * (rows[0][1] - rows[0][0])
        scratch += [
            pltpu.VMEM((n * keys, columns), jnp.bfloat16),
            pltpu.VMEM((slots, reach.shape[1]), jnp.int32),
        ]
    if last:
        shape = (q_dev, total // q_dev * width)
        out_shape, out_specs = jax.ShapeDtypeStruct(shape, jnp.bfloat16), pl.BlockSpec(memory_space=pl.ANY)
        scratch = [pltpu.VMEM(shape, jnp.bfloat16), pltpu.SemaphoreType.DMA((total // lanes,))] + scratch
    else:
        out_shape = (
            jax.ShapeDtypeStruct((8, total), jnp.float32),
            jax.ShapeDtypeStruct((width + 16, total), jnp.float32),
        )
        out_specs = (VMEM, VMEM)
    args = [qs, reach, *pieces, *(state or ())]
    n_keys = keys * n
    return pl.pallas_call(
        functools.partial(part_kernel, rows, q_dev, lanes, state is not None, last, pack),
        out_shape=out_shape,
        in_specs=[VMEM] * len(args),
        out_specs=out_specs,
        scratch_shapes=scratch,
        compiler_params=PARAMS,
        cost_estimate=pl.CostEstimate(
            flops=8 * total * width * n_keys, bytes_accessed=4 * n_keys * width, transcendentals=total * n_keys
        ),
        name="part_last" if last else "part",
    )(*args)


def shards(n_pb, n_ka, queries, keys, values, query_pos, key_pos, block_mask):
    q_dev, width = queries.shape[0], keys.shape[1]
    n_devices = n_pb * n_ka
    groups, core = step_groups(n_pb, n_ka)

    def send(x, step):
        return swap(x, step, n_devices)

    x, steps = jnp.concatenate([keys, values], 1), [0]
    for group in groups[:-1]:
        x = jnp.concatenate([x] + [send(x, step) for step in group], 0)
        steps = [s ^ g for g in [0] + group for s in steps]
    n = len(steps)
    last = [0] + groups[-1]
    steps = [s ^ g ^ c for c in (0, core) for g in last for s in steps]
    tiles = [(s % n_ka) * n_pb + s // n_ka for s in steps]
    qs, reach = plan(queries, query_pos, key_pos, block_mask, n_pb, n_ka, tiles, width)
    x, qs, reach = lax.optimization_barrier((x, qs, reach))

    mine = [x] + [send(x, step) for step in groups[-1]]
    m = len(mine)
    rows = [(j * n, (j + 1) * n) for j in range(2 * m)]

    def add(state, some, last=False):
        pieces = [piece for piece, _ in some]
        return part(qs, reach, pieces, [rows[j] for _, j in some], q_dev, state, last)

    def after(arrays, state):
        return lax.optimization_barrier((arrays, state))

    state = add(None, [(x, 0)])
    some = []
    if m > 2:
        mine[1], state = after(mine[1], state)
        some = [(send(mine[1], core), m + 1)]
    some = [(send(x, core), m)] + some
    if m > 2:
        state = add(state, [(mine[1], 1)])
    k = min(2, m - 1)
    y, state = after(mine[k], state)
    rest = [y] + mine[k + 1 :]
    others = [send(y, core) for y in rest]
    state = add(state, some + [(rest[0], k)])
    some = [(y, k + 1 + j) for j, y in enumerate(rest[1:])]
    return add(state, some + [(y, m + k + j) for j, y in enumerate(others)], last=True)


def solution(mesh):
    n_pb, n_ka = mesh.shape["pb"], mesh.shape["ka"]
    return jax.shard_map(
        functools.partial(shards, n_pb, n_ka),
        mesh=mesh,
        in_specs=(
            P(("pb", "ka"), None),
            P(("ka", "pb"), None),
            P(("ka", "pb"), None),
            P(),
            P(),
            P(),
        ),
        out_specs=P(("pb", "ka"), None),
        check_vma=False,
    )
```
